32 devices in a mesh: gx: 4 (over y, core), gy: 8 (over z, x).
Axes of the slice: x: 2, y: 2, z: 4, core: 2. Of those that a mesh axis runs over, the one named last changes fastest.
Arguments:
- motion: float32 [384, 128, 3, 512], P('gx', 'gy'), may hold values from -40 to 40
- time_sketch: float32 [512, 128], replicated, may hold values from -0.25 to 0.25
- x_sketch: float32 [384, 128], replicated, may hold values from -0.3125 to 0.3125
Outputs:
- time_core: float32 [384, 128, 3, 128], P('gx', 'gy')
- x_core: float32 [128, 3, 128, 128], P('gy', None, 'gx')
The draws below stay inside these ranges and needn't reach their ends.
All inputs are finite; a program needn't handle non-finite values.
Results may differ from the reference program's by a relative error of at most 0.0003.
Values sent between devices are 32-bit elements; how exact they have to be, the bound alone decides.
No kernel may reach another device: no remote copies, remote signals or barrier semaphores. Data moves between devices by JAX's collectives and lax.ppermute only.
A program may use at most 128 MiB of HBM per device.

```python
import math
import jax
import jax.numpy as jnp
from jax import lax

COMP = 3
STEPS = 512
RANK_T = 128
RANK_X = 128
POWER = 3
NX = 384
NY = 128


def draw_motion(key, part):
    key_rough = jax.random.fold_in(key, 11)
    key_wave = jax.random.fold_in(key, 12)
    xpos = jnp.arange(NX, dtype=jnp.float32) / NX
    ypos = jnp.arange(NY, dtype=jnp.float32) / NY
    trend = jnp.exp(0.5 * math.log(3.0) * (xpos[:, None] + ypos[None, :]))
    rough = jnp.exp(jax.random.uniform(key_rough, (NX, NY), jnp.float32, math.log(0.5), math.log(2.0)))
    amp = trend * rough
    comp_index = jnp.arange(COMP, dtype=jnp.float32)
    comp_scale = 1.0 - 0.4 * (comp_index == COMP - 1).astype(jnp.float32)
    wave = jax.random.normal(key_wave, (NX, NY, COMP, STEPS), jnp.float32)
    values = amp[:, :, None, None] * comp_scale[None, None, :, None] * wave
    return jnp.clip(values, -40.0, 40.0)


def scatter_about(stream_key, extent, width, bound, kind=jnp.bfloat16):
    result = jax.random.normal(stream_key, extent, jnp.float32) * width
    return jnp.minimum(jnp.maximum(result, -bound), bound).astype(kind)


def setup_inputs(seed: int = 0) -> dict:
    keys = jax.random.split(jax.random.key(seed), 4)
    motion = draw_motion(jax.random.fold_in(keys[3], 71), 0)
    time_sketch = scatter_about(keys[1], (STEPS, RANK_T), STEPS ** -0.5, 0.25, jnp.float32)
    x_sketch = scatter_about(keys[2], (NX, RANK_X), NX ** -0.5, 0.3125, jnp.float32)
    return {"motion": motion, "time_sketch": time_sketch, "x_sketch": x_sketch}


HIGH = lax.Precision.HIGHEST

def orthonormal(mat):
    gram = jnp.dot(mat.T.astype(jnp.float32), mat.astype(jnp.float32), precision=HIGH, preferred_element_type=jnp.float32)
    lower = jnp.linalg.cholesky(gram)
    return jax.scipy.linalg.solve_triangular(lower, mat.T, lower=True).T

def leading_basis(gram, sketch):
    basis = orthonormal(jnp.dot(gram.astype(jnp.float32), sketch.astype(jnp.float32), precision=HIGH, preferred_element_type=jnp.float32))
    for step in range(POWER - 1):
        basis = orthonormal(jnp.dot(gram.astype(jnp.float32), basis.astype(jnp.float32), precision=HIGH, preferred_element_type=jnp.float32))
    return basis

def reference(motion, time_sketch, x_sketch):
    flat = motion.reshape(NX * NY * COMP, STEPS)
    time_gram = lax.dot_general(flat.astype(jnp.float32), flat.astype(jnp.float32), (((0,), (0,)), ((), ())), precision=HIGH, preferred_element_type=jnp.float32) / (NX * NY * COMP)
    time_basis = leading_basis(time_gram, time_sketch)
    time_core = jnp.dot(flat.astype(jnp.float32), time_basis.astype(jnp.float32), precision=HIGH, preferred_element_type=jnp.float32)
    cols = time_core.reshape(NX, NY * COMP * RANK_T)
    x_gram = jnp.dot(cols.astype(jnp.float32), cols.T.astype(jnp.float32), precision=HIGH, preferred_element_type=jnp.float32) / (NY * COMP * RANK_T)
    x_basis = leading_basis(x_gram, x_sketch)
    x_core = lax.dot_general(cols.astype(jnp.float32), x_basis.astype(jnp.float32), (((0,), (0,)), ((), ())), precision=HIGH, preferred_element_type=jnp.float32)
    return (time_core.reshape(NX, NY, COMP, RANK_T), x_core.reshape(NY, COMP, RANK_T, RANK_X))
```

```python
import jax
import jax.numpy as jnp
from jax import lax
from jax.sharding import PartitionSpec as P

POWER = 3
BLOCK = 128
HIGH = lax.Precision.HIGH
HIGHEST = lax.Precision.HIGHEST


def exchange(value, axis, mask):
    size = lax.axis_size(axis)
    return lax.ppermute(value, axis, [(i, i ^ mask) for i in range(size)])


def bits_of(size):
    bits = []
    mask = 1
    while mask < size:
        bits.append(mask)
        mask *= 2
    return bits


def sum_all(buf):
    steps = [("gx", m) for m in bits_of(lax.axis_size("gx"))]
    steps += [("gy", m) for m in bits_of(lax.axis_size("gy"))]
    halved = []
    for axis, mask in steps:
        rows = buf.shape[0]
        if rows % 16:
            buf = buf + exchange(buf, axis, mask)
            continue
        upper = (lax.axis_index(axis) & mask) != 0
        low, high = buf[: rows // 2], buf[rows // 2 :]
        got = exchange(jnp.where(upper, low, high), axis, mask)
        buf = jnp.where(upper, high, low) + got
        halved.append((axis, mask, upper))
    for axis, mask, upper in reversed(halved):
        got = exchange(buf, axis, mask)
        buf = jnp.where(upper, jnp.concatenate([got, buf]), jnp.concatenate([buf, got]))
    return buf


def sum_gram(partial):
    n = partial.shape[0] // BLOCK
    pairs = [(i, j) for i in range(n) for j in range(i, n)]

    def block(i, j):
        return partial[i * BLOCK : (i + 1) * BLOCK, j * BLOCK : (j + 1) * BLOCK]

    packed = sum_all(jnp.concatenate([block(i, j) for i, j in pairs]))
    at = {pair: packed[k * BLOCK : (k + 1) * BLOCK] for k, pair in enumerate(pairs)}
    return jnp.concatenate(
        [
            jnp.concatenate([at[i, j] if i <= j else at[j, i].T for j in range(n)], axis=1)
            for i in range(n)
        ]
    )


def orthonormal(mat):
    gram = jnp.dot(mat.T, mat, precision=HIGHEST, preferred_element_type=jnp.float32)
    lower = jnp.linalg.cholesky(gram)
    return jax.scipy.linalg.solve_triangular(lower, mat.T, lower=True).T


def leading_basis(partial_value, sketch):
    gram = sum_gram(partial_value)

    def product(mat):
        return jnp.dot(gram, mat, precision=HIGHEST, preferred_element_type=jnp.float32)

    basis = orthonormal(product(sketch))
    for step in range(POWER - 1):
        basis = orthonormal(product(basis))
    return basis


def shards(motion, time_sketch, x_sketch):
    cx_local, cy_local, comps, steps = motion.shape
    n_gx = lax.axis_size("gx")
    n_gy = lax.axis_size("gy")
    flat = motion.transpose(0, 2, 1, 3).reshape(cx_local * comps * cy_local, steps)
    partial_value = lax.dot_general(
        flat, flat, (((0,), (0,)), ((), ())), precision=HIGH, preferred_element_type=jnp.float32
    )
    partial_value = partial_value / (cx_local * n_gx * cy_local * n_gy * comps)
    time_basis = leading_basis(partial_value, time_sketch)
    ranks = time_basis.shape[1]
    share = ranks // n_gx
    core = jnp.dot(flat, time_basis, precision=HIGH, preferred_element_type=jnp.float32)
    time_core = core.reshape(cx_local, comps, cy_local, ranks).transpose(0, 2, 1, 3)

    columns = comps * cy_local * share
    parts = core.reshape(cx_local, comps * cy_local, n_gx, share).transpose(2, 0, 1, 3)
    parts = parts.reshape(n_gx, cx_local, columns)
    mine = lax.axis_index("gx")
    cols = jnp.zeros((n_gx, cx_local, columns), jnp.float32)
    for mask in range(n_gx):
        part = lax.dynamic_index_in_dim(parts, mine ^ mask, 0, keepdims=False)
        if mask:
            part = exchange(part, "gx", mask)
        cols = lax.dynamic_update_index_in_dim(cols, part, mine ^ mask, 0)
    cols = cols.reshape(n_gx * cx_local, columns)

    x_partial = jnp.dot(cols, cols.T, precision=HIGH, preferred_element_type=jnp.float32) / (
        cy_local * n_gy * comps * ranks
    )
    x_basis = leading_basis(x_partial, x_sketch)
    x_core = lax.dot_general(
        cols, x_basis, (((0,), (0,)), ((), ())), precision=HIGH, preferred_element_type=jnp.float32
    )
    x_core = x_core.reshape(comps, cy_local, share, x_basis.shape[1]).transpose(1, 0, 2, 3)
    return (time_core, x_core)


def solution(mesh):
    in_specs = (P("gx", "gy", None, None), P(), P())
    out_specs = (P("gx", "gy", None, None), P("gy", None, "gx", None))
    return jax.shard_map(shards, mesh=mesh, in_specs=in_specs, out_specs=out_specs, check_vma=False)
```

```python
import jax
import jax.numpy as jnp
from jax import lax
from jax.experimental import pallas as pl
from jax.experimental.pallas import tpu as pltpu
from jax.sharding import PartitionSpec as P

HIGH = lax.Precision.HIGH
BLOCK = 128
PANEL = 16
POWER = 3
HIGHEST = lax.Precision.HIGHEST


def dot(a, b, ca, cb):
    return lax.dot_general(
        a, b, (((ca,), (cb,)), ((), ())), precision=HIGHEST, preferred_element_type=jnp.float32
    )


def factor_panel(work, splat, rows, start):
    ranks = work.shape[0]
    here = pl.ds(start, PANEL)
    for i in range(PANEL):
        splat[i] = jnp.broadcast_to(work[here, start + i : start + i + 1], (PANEL, ranks))
    entry = {(k, i): splat[i, k : k + 1, :] for i in range(PANEL) for k in range(i, PANEL)}
    done = []
    for i in range(PANEL):
        scale = lax.rsqrt(entry[i, i])
        low = {k: entry[k, i] * scale for k in range(i + 1, PANEL)}
        for k in range(i + 1, PANEL):
            for j in range(i + 1, k + 1):
                entry[k, j] = entry[k, j] - low[k] * low[j]
        for k in range(i + 1, PANEL):
            entry[k, i] = low[k]
        halves = []
        for half in range(2):
            row = work[start + i : start + i + 1, half * ranks : (half + 1) * ranks]
            for k in range(i):
                row = row - entry[i, k] * done[k][half]
            row = row * scale
            rows[start + i : start + i + 1, half * ranks : (half + 1) * ranks] = row
            halves.append(row)
        done.append(halves)


def basis_kernel(packed_ref, sketch_ref, out_ref, gram, prod, work, rows, splat):
    size = sketch_ref.shape[0]
    ranks = sketch_ref.shape[1]
    n = size // BLOCK
    at = 0
    for i in range(n):
        for j in range(i, n):
            block = packed_ref[at * BLOCK : (at + 1) * BLOCK, :]
            gram[i * BLOCK : (i + 1) * BLOCK, j * BLOCK : (j + 1) * BLOCK] = block
            if i != j:
                gram[j * BLOCK : (j + 1) * BLOCK, i * BLOCK : (i + 1) * BLOCK] = block.T
            at += 1
    prod[...] = dot(sketch_ref[...], gram[...], 0, 0)

    def orthonormal(step, carry):
        @pl.when(step > 0)
        def _():
            prod[...] = dot(out_ref[...], gram[...], 1, 0)

        value = prod[...]
        work[:, :ranks] = dot(value, value, 1, 1)
        row = lax.broadcasted_iota(jnp.int32, (ranks, ranks), 0)
        col = lax.broadcasted_iota(jnp.int32, (ranks, ranks), 1)
        work[:, ranks:] = jnp.where(row == col, 1.0, 0.0)
        for start in range(0, ranks, PANEL):
            factor_panel(work, splat, rows, start)
            if start + PANEL < ranks:
                panel = rows[start : start + PANEL, :]
                rest = start + PANEL
                work[rest:, :] = work[rest:, :] - dot(panel[:, rest:ranks], panel, 0, 0)
        out_ref[...] = dot(rows[:, ranks:], prod[...], 1, 0)
        return carry

    lax.fori_loop(0, POWER, orthonormal, 0)


def leading_basis(packed, sketch):
    size, ranks = sketch.shape
    return pl.pallas_call(
        basis_kernel,
        out_shape=jax.ShapeDtypeStruct((ranks, size), jnp.float32),
        in_specs=[pl.BlockSpec(memory_space=pltpu.VMEM)] * 2,
        out_specs=pl.BlockSpec(memory_space=pltpu.VMEM),
        scratch_shapes=[
            pltpu.VMEM((size, size), jnp.float32),
            pltpu.VMEM((ranks, size), jnp.float32),
            pltpu.VMEM((ranks, 2 * ranks), jnp.float32),
            pltpu.VMEM((ranks, 2 * ranks), jnp.float32),
            pltpu.VMEM((PANEL, PANEL, ranks), jnp.float32),
        ],
        compiler_params=pltpu.CompilerParams(vmem_limit_bytes=32 * 2**20),
        name="leading_basis",
    )(packed, sketch)


def exchange(value, axis, mask):
    size = lax.axis_size(axis)
    return lax.ppermute(value, axis, [(i, i ^ mask) for i in range(size)])


def bits_of(size):
    bits = []
    mask = 1
    while mask < size:
        bits.append(mask)
        mask *= 2
    return bits


def sum_all(buf):
    steps = [("gx", m) for m in bits_of(lax.axis_size("gx"))]
    steps += [("gy", m) for m in bits_of(lax.axis_size("gy"))]
    halved = []
    for axis, mask in steps:
        rows = buf.shape[0]
        if rows % 16 or rows <= 160:
            buf = buf + exchange(buf, axis, mask)
            continue
        upper = (lax.axis_index(axis) & mask) != 0
        low, high = buf[: rows // 2], buf[rows // 2 :]
        got = exchange(jnp.where(upper, low, high), axis, mask)
        buf = jnp.where(upper, high, low) + got
        halved.append((axis, mask, upper))
    for axis, mask, upper in reversed(halved):
        got = exchange(buf, axis, mask)
        buf = jnp.where(upper, jnp.concatenate([got, buf]), jnp.concatenate([buf, got]))
    return buf


def sum_gram(partial):
    n = partial.shape[0] // BLOCK
    pairs = [(i, j) for i in range(n) for j in range(i, n)]

    def block(i, j):
        return partial[i * BLOCK : (i + 1) * BLOCK, j * BLOCK : (j + 1) * BLOCK]

    return sum_all(jnp.concatenate([block(i, j) for i, j in pairs]))


def shards(motion, time_sketch, x_sketch):
    cx_local, cy_local, comps, steps = motion.shape
    n_gx = lax.axis_size("gx")
    n_gy = lax.axis_size("gy")
    flat = motion.transpose(0, 2, 1, 3).reshape(cx_local * comps * cy_local, steps)
    partial_value = lax.dot_general(
        flat, flat, (((0,), (0,)), ((), ())), precision=HIGH, preferred_element_type=jnp.float32
    )
    partial_value = partial_value / (cx_local * n_gx * cy_local * n_gy * comps)
    time_basis = leading_basis(sum_gram(partial_value), time_sketch)
    ranks = time_basis.shape[0]
    share = ranks // n_gx
    core = jnp.dot(flat, time_basis.T, precision=HIGH, preferred_element_type=jnp.float32)
    time_core = core.reshape(cx_local, comps, cy_local, ranks).transpose(0, 2, 1, 3)

    columns = comps * cy_local * share
    parts = core.reshape(cx_local, comps * cy_local, n_gx, share).transpose(2, 0, 1, 3)
    parts = parts.reshape(n_gx, cx_local, columns)
    mine = lax.axis_index("gx")
    cols = jnp.zeros((n_gx, cx_local, columns), jnp.float32)
    for mask in range(n_gx):
        part = lax.dynamic_index_in_dim(parts, mine ^ mask, 0, keepdims=False)
        if mask:
            part = exchange(part, "gx", mask)
        cols = lax.dynamic_update_index_in_dim(cols, part, mine ^ mask, 0)
    cols = cols.reshape(n_gx * cx_local, columns)

    x_partial = jnp.dot(cols, cols.T, precision=HIGH, preferred_element_type=jnp.float32) / (
        cy_local * n_gy * comps * ranks
    )
    x_basis = leading_basis(sum_gram(x_partial), x_sketch)
    x_core = lax.dot_general(
        cols, x_basis, (((0,), (1,)), ((), ())), precision=HIGH, preferred_element_type=jnp.float32
    )
    x_core = x_core.reshape(comps, cy_local, share, x_basis.shape[0]).transpose(1, 0, 2, 3)
    return (time_core, x_core)


def solution(mesh):
    in_specs = (P("gx", "gy", None, None), P(), P())
    out_specs = (P("gx", "gy", None, None), P("gy", None, "gx", None))
    return jax.shard_map(shards, mesh=mesh, in_specs=in_specs, out_specs=out_specs, check_vma=False)
```

```python
import jax
import jax.numpy as jnp
from jax import lax
from jax.experimental import pallas as pl
from jax.experimental.pallas import tpu as pltpu
from jax.sharding import PartitionSpec as P

BLOCK = 128
PANEL = 16
POWER = 3
HIGHEST = lax.Precision.HIGHEST
VMEM = pl.BlockSpec(memory_space=pltpu.VMEM)
LIMIT = pltpu.CompilerParams(vmem_limit_bytes=40 * 2**20)


def dot(a, b, ca, cb):
    return lax.dot_general(
        a, b, (((ca,), (cb,)), ((), ())), precision=HIGHEST, preferred_element_type=jnp.float32
    )


def factor_panel(work, splat, rows, start):
    ranks = work.shape[0]
    here = pl.ds(start, PANEL)
    for i in range(PANEL):
        splat[i] = jnp.broadcast_to(work[here, start + i : start + i + 1], (PANEL, ranks))
    entry = {(k, i): splat[i, k : k + 1, :] for i in range(PANEL) for k in range(i, PANEL)}
    done = []
    for i in range(PANEL):
        scale = lax.rsqrt(entry[i, i])
        low = {k: entry[k, i] * scale for k in range(i + 1, PANEL)}
        for k in range(i + 1, PANEL):
            for j in range(i + 1, k + 1):
                entry[k, j] = entry[k, j] - low[k] * low[j]
        for k in range(i + 1, PANEL):
            entry[k, i] = low[k]
        halves = []
        for half in range(2):
            row = work[start + i : start + i + 1, half * ranks : (half + 1) * ranks]
            for k in range(i):
                row = row - entry[i, k] * done[k][half]
            row = row * scale
            rows[start + i : start + i + 1, half * ranks : (half + 1) * ranks] = row
            halves.append(row)
        done.append(halves)


def basis_kernel(packed_ref, sketch_ref, out_ref, gram, prod, work, rows, splat):
    size = sketch_ref.shape[0]
    ranks = sketch_ref.shape[1]
    n = size // BLOCK
    at = 0
    for i in range(n):
        for j in range(i, n):
            block = packed_ref[at * BLOCK : (at + 1) * BLOCK, :]
            gram[i * BLOCK : (i + 1) * BLOCK, j * BLOCK : (j + 1) * BLOCK] = block
            if i != j:
                gram[j * BLOCK : (j + 1) * BLOCK, i * BLOCK : (i + 1) * BLOCK] = block.T
            at += 1
    prod[...] = dot(sketch_ref[...], gram[...], 0, 0)

    def orthonormal(step, carry):
        @pl.when(step > 0)
        def _():
            prod[...] = dot(out_ref[...], gram[...], 1, 0)

        value = prod[...]
        work[:, :ranks] = dot(value, value, 1, 1)
        row = lax.broadcasted_iota(jnp.int32, (ranks, ranks), 0)
        col = lax.broadcasted_iota(jnp.int32, (ranks, ranks), 1)
        work[:, ranks:] = jnp.where(row == col, 1.0, 0.0)
        for start in range(0, ranks, PANEL):
            factor_panel(work, splat, rows, start)
            if start + PANEL < ranks:
                panel = rows[start : start + PANEL, :]
                rest = start + PANEL
                work[rest:, :] = work[rest:, :] - dot(panel[:, rest:ranks], panel, 0, 0)
        out_ref[...] = dot(rows[:, ranks:], prod[...], 1, 0)
        return carry

    lax.fori_loop(0, POWER, orthonormal, 0)


def leading_basis(packed, sketch):
    size, ranks = sketch.shape
    return pl.pallas_call(
        basis_kernel,
        out_shape=jax.ShapeDtypeStruct((ranks, size), jnp.float32),
        in_specs=[pl.BlockSpec(memory_space=pltpu.VMEM)] * 2,
        out_specs=pl.BlockSpec(memory_space=pltpu.VMEM),
        scratch_shapes=[
            pltpu.VMEM((size, size), jnp.float32),
            pltpu.VMEM((ranks, size), jnp.float32),
            pltpu.VMEM((ranks, 2 * ranks), jnp.float32),
            pltpu.VMEM((ranks, 2 * ranks), jnp.float32),
            pltpu.VMEM((PANEL, PANEL, ranks), jnp.float32),
        ],
        compiler_params=pltpu.CompilerParams(vmem_limit_bytes=32 * 2**20),
        name="leading_basis",
    )(packed, sketch)


def split(value):
    high = value.astype(jnp.bfloat16)
    return high, (value - high.astype(jnp.float32)).astype(jnp.bfloat16)


def pass_dot(a, b, ca, cb):
    return lax.dot_general(a, b, (((ca,), (cb,)), ((), ())), preferred_element_type=jnp.float32)


def pack_triangle(square, cross, out_ref, scale):
    n = square.shape[0] // BLOCK
    at = 0
    for i in range(n):
        for j in range(i, n):
            rows, cols = pl.ds(i * BLOCK, BLOCK), pl.ds(j * BLOCK, BLOCK)
            total = square[rows, cols] + (cross[rows, cols] + cross[cols, rows].T)
            out_ref[at * BLOCK : (at + 1) * BLOCK, :] = total * scale
            at += 1


def packed_rows(size):
    n = size // BLOCK
    return n * (n + 1) // 2 * BLOCK


def time_gram(flat, scale):
    rows, steps = flat.shape
    block = rows // 6
    half = steps // 2

    def kernel(flat_ref, out_ref, square, cross):
        at = pl.program_id(0)

        @pl.when(at == 0)
        def _():
            square[...] = jnp.zeros_like(square)
            cross[...] = jnp.zeros_like(cross)

        high, low = split(flat_ref[...])
        for i in range(2):
            here = slice(i * half, (i + 1) * half)
            square[here, i * half :] += pass_dot(high[:, here], high[:, i * half :], 0, 0)
            cross[here, :] += pass_dot(high[:, here], low, 0, 0)

        @pl.when(at == pl.num_programs(0) - 1)
        def _():
            pack_triangle(square, cross, out_ref, scale)

    return pl.pallas_call(
        kernel,
        grid=(6,),
        out_shape=jax.ShapeDtypeStruct((packed_rows(steps), BLOCK), jnp.float32),
        in_specs=[pl.BlockSpec((block, steps), lambda i: (i, 0))],
        out_specs=pl.BlockSpec((packed_rows(steps), BLOCK), lambda i: (0, 0)),
        scratch_shapes=[pltpu.VMEM((steps, steps), jnp.float32)] * 2,
        compiler_params=LIMIT,
        name="time_gram",
    )(flat)


def project(flat, basis, n_gx):
    sites, inner, steps = flat.shape
    ranks = basis.shape[0]
    share = ranks // n_gx
    groups = inner // n_gx
    block = 16
    columns = inner * share

    def kernel(flat_ref, basis_ref, core_ref, *rest):
        part_refs, (core, parts) = rest[:n_gx], rest[n_gx:]
        high, low = split(flat_ref[...].reshape(block * inner, steps))
        basis_high, basis_low = split(basis_ref[...])
        wide = pass_dot(high, jnp.concatenate([basis_high, basis_low]), 1, 1)
        value = wide[:, :ranks] + (wide[:, ranks:] + pass_dot(low, basis_high, 1, 1))
        core[...] = value
        core_ref[...] = value.reshape(block, inner, ranks)
        lane = lax.broadcasted_iota(jnp.int32, (block, ranks), 1) // share
        for group in range(groups):
            rows = [
                core[pl.ds(group * n_gx + y, block, stride=inner), :] for y in range(n_gx)
            ]
            for owner in range(n_gx):
                out = rows[owner]
                for y in range(n_gx):
                    if y != owner:
                        moved = pltpu.roll(rows[y], (y - owner) % n_gx * share, 1)
                        out = jnp.where(lane == y, moved, out)
                parts[owner, :, group * ranks : (group + 1) * ranks] = out
        mine = lax.axis_index("gx")
        for mask in range(n_gx):
            part_refs[mask][...] = parts[mine ^ mask]

    part = jax.ShapeDtypeStruct((sites, columns), jnp.float32)
    return pl.pallas_call(
        kernel,
        grid=(sites // block,),
        out_shape=[jax.ShapeDtypeStruct((sites, inner, ranks), jnp.float32)] + [part] * n_gx,
        in_specs=[
            pl.BlockSpec((block, inner, steps), lambda i: (i, 0, 0)),
            pl.BlockSpec((ranks, steps), lambda i: (0, 0)),
        ],
        out_specs=[pl.BlockSpec((block, inner, ranks), lambda i: (i, 0, 0))]
        + [pl.BlockSpec((block, columns), lambda i: (i, 0))] * n_gx,
        scratch_shapes=[
            pltpu.VMEM((block * inner, ranks), jnp.float32),
            pltpu.VMEM((n_gx, block, columns), jnp.float32),
        ],
        compiler_params=LIMIT,
        name="project_time",
    )(flat, basis)


def x_gram(parts, scale):
    n_gx = len(parts)
    sites, columns = parts[0].shape
    size = n_gx * sites

    def kernel(*refs):
        part_refs = refs[:n_gx]
        cols_ref, out_ref, square, cross, sems = refs[n_gx:]
        mine = lax.axis_index("gx")
        copies = []
        for mask in range(n_gx):
            rows = pl.ds(pl.multiple_of((mine ^ mask) * sites, 8), sites)
            copies.append(
                pltpu.make_async_copy(part_refs[mask], cols_ref.at[rows, :], sems.at[mask])
            )
            copies[-1].start()
        for copy in copies:
            copy.wait()
        high, low = split(cols_ref[...])
        square[...] = pass_dot(high, high, 1, 1)
        cross[...] = pass_dot(high, low, 1, 1)
        pack_triangle(square, cross, out_ref, scale)

    return pl.pallas_call(
        kernel,
        out_shape=[
            jax.ShapeDtypeStruct((size, columns), jnp.float32),
            jax.ShapeDtypeStruct((packed_rows(size), BLOCK), jnp.float32),
        ],
        in_specs=[pl.BlockSpec(memory_space=pl.ANY)] * n_gx,
        out_specs=[VMEM, VMEM],
        scratch_shapes=[pltpu.VMEM((size, size), jnp.float32)] * 2
        + [pltpu.SemaphoreType.DMA((n_gx,))],
        compiler_params=LIMIT,
        name="x_gram",
    )(*parts)


def project_x(cols, basis, comps, cy_local, share):
    ranks = basis.shape[0]
    per_block = BLOCK // share
    blocks = cy_local // per_block

    def kernel(cols_ref, basis_ref, out_ref):
        high, low = split(cols_ref[...])
        basis_high, basis_low = split(basis_ref[...])
        value = pass_dot(basis_high, high, 1, 0) + (
            pass_dot(basis_high, low, 1, 0) + pass_dot(basis_low, high, 1, 0)
        )
        for c in range(comps):
            for b in range(blocks):
                at = (c * blocks + b) * BLOCK
                tile = value[:, at : at + BLOCK].T.reshape(per_block, share, ranks)
                out_ref[b * per_block : (b + 1) * per_block, c] = tile

    return pl.pallas_call(
        kernel,
        out_shape=jax.ShapeDtypeStruct((cy_local, comps, share, ranks), jnp.float32),
        in_specs=[VMEM, VMEM],
        out_specs=VMEM,
        compiler_params=LIMIT,
        name="project_x",
    )(cols, basis)


AXES = ("gx", "gy")


def combos(masks):
    found = [0]
    for mask in masks:
        found += [mask ^ old for old in found]
    return found


def exchange(value, mask):
    size = lax.axis_size(AXES)
    return lax.ppermute(value, AXES, [(i, i ^ mask) for i in range(size)])


def sum_all(buf):
    n_gx, n_gy = lax.axis_size("gx"), lax.axis_size("gy")
    me = lax.axis_index("gx") * n_gy + lax.axis_index("gy")
    bits = [1 << b for b in range((n_gx * n_gy).bit_length() - 1)]
    groups = [[n_gy], [1, 2 * n_gy]]
    later = [m for m in bits if m not in (n_gy, 1, 2 * n_gy)]
    shared = []
    for group in groups:
        masks = combos(group)
        rows = buf.shape[0] // len(masks)
        place = sum(jnp.where(me & m, 1 << b, 0) for b, m in enumerate(group))
        total = lax.dynamic_slice_in_dim(buf, place * rows, rows)
        for b, mask in enumerate(masks):
            if b:
                total = total + exchange(
                    lax.dynamic_slice_in_dim(buf, (place ^ b) * rows, rows), mask
                )
        shared.append((masks, place, rows))
        buf = total
    for mask in later:
        buf = buf + exchange(buf, mask)
    for masks, place, rows in reversed(shared):
        whole = jnp.zeros((rows * len(masks), buf.shape[1]), buf.dtype)
        for b, mask in enumerate(masks):
            piece = exchange(buf, mask) if b else buf
            whole = lax.dynamic_update_slice_in_dim(whole, piece, (place ^ b) * rows, 0)
        buf = whole
    return buf


def shards(motion, time_sketch, x_sketch):
    cx_local, cy_local, comps, steps = motion.shape
    n_gx = lax.axis_size("gx")
    n_gy = lax.axis_size("gy")
    ranks = time_sketch.shape[1]
    share = ranks // n_gx
    inner = comps * cy_local
    flat = motion.transpose(0, 2, 1, 3).reshape(cx_local, inner, steps)

    scale = 1.0 / (cx_local * n_gx * cy_local * n_gy * comps)
    packed = time_gram(flat.reshape(cx_local * inner, steps), scale)
    time_basis = leading_basis(sum_all(packed), time_sketch)
    core, *parts = project(flat, time_basis, n_gx)
    time_core = core.reshape(cx_local, comps, cy_local, ranks).transpose(0, 2, 1, 3)

    parts = [exchange(part, mask * n_gy) if mask else part for mask, part in enumerate(parts)]
    cols, packed = x_gram(parts, 1.0 / (cy_local * n_gy * comps * ranks))
    x_basis = leading_basis(sum_all(packed), x_sketch)
    return (time_core, project_x(cols, x_basis, comps, cy_local, share))


def solution(mesh):
    in_specs = (P("gx", "gy", None, None), P(), P())
    out_specs = (P("gx", "gy", None, None), P("gy", None, "gx", None))
    return jax.shard_map(shards, mesh=mesh, in_specs=in_specs, out_specs=out_specs, check_vma=False)
```
